256 devices in a mesh: seq: 64 (over z, x, y_hi), heads: 4 (over y_lo, core).
Axes of the slice: x: 4, y: 4 (y_hi: 2, y_lo: 2; y = y_hi * 2 + y_lo), z: 8, core: 2. Of those that a mesh axis runs over, the one named last changes fastest.
Arguments:
- query: bfloat16 [16384, 1024], P('seq', 'heads'), may hold values from -6 to 6
- key_rows: bfloat16 [16384, 128], P('seq'), may hold values from -6 to 6
- head_value_rows: bfloat16 [16384, 128], P('seq'), may hold values from -6 to 6
- output: bfloat16 [16384, 1024], P('seq', 'heads'), may hold values from -6 to 6
- out_grad: bfloat16 [16384, 1024], P('seq', 'heads'), may hold values from -0.59765625 to 0.59765625
- logsumexp: float32 [8, 16384], P('heads', 'seq'), as said below
- block_pos: int32 [128], P('seq'), may hold values from 0 to 127, as said below
Outputs:
- query_grad: bfloat16 [16384, 1024], P('seq', 'heads')
- key_grad: bfloat16 [16384, 128], P('seq')
- value_grad: bfloat16 [16384, 128], P('seq')
The draws below stay inside these ranges and needn't reach their ends.
Inputs may be any that keep to these rules, and one draw needn't show every extreme that they name: `block_pos`: a permutation of the half-block numbers in which stored half-blocks 2 d and 2 d + 1 hold sequence half-blocks b and 127 - b for some b < 64. `logsumexp`: an input offset near log(1.65 (pos + 1)) of the row's sequence position, not recomputed from the scores.
All inputs are finite; a program needn't handle non-finite values.
Results may differ from the reference program's by a relative error of at most 0.0052.
Values may be sent and summed in bfloat16 or wider, within the bound.
No kernel may reach another device: no remote copies, remote signals or barrier semaphores. Data moves between devices by JAX's collectives and lax.ppermute only.
A program may use at most 64 MiB of HBM per device.

```python
import math
import jax
import jax.numpy as jnp
from jax import lax

DH = 128
QH = 8
HALF = 128
BLOCKS = 128
SEQLEN = 16384


def shared_order(key):
    pairs = BLOCKS // 2
    lower = jax.random.permutation(key, pairs).astype(jnp.int32)
    upper = (BLOCKS - 1 - lower).astype(jnp.int32)
    return jnp.stack([lower, upper], axis=1).reshape(BLOCKS).astype(jnp.int32)


def draw_block_pos(key, part):
    return shared_order(key)


def draw_logsumexp(key, part):
    order = shared_order(key)
    key = jax.random.fold_in(key, 7)
    tokpos = (order[:, None] * HALF + jnp.arange(HALF, dtype=jnp.int32)[None, :]).reshape(-1).astype(jnp.float32)
    base = jnp.log(1.65 * (tokpos + 1.0))
    noise = jax.random.uniform(key, (QH, SEQLEN), jnp.float32, -0.3, 0.3)
    return base[None, :] + noise


def steps_of(own_key, shape, cuts, least, largest):
    factor_of = 1.0
    for dim, blocks in cuts:
        draws = jax.random.uniform(jax.random.fold_in(jax.random.fold_in(own_key, 6), dim), (blocks,), jnp.float32, least / len(cuts), largest / len(cuts))
        factor_of = factor_of * jnp.repeat(jnp.exp(draws), shape[dim] // blocks).reshape((-1,) + (1,) * (len(shape) - 1 - dim))
    return factor_of


def bell_draw(key, shape, scale, most, shards=(), kind=jnp.bfloat16):
    result = jax.random.normal(key, shape, jnp.float32) * scale
    if len(shards) > 0:
        result = steps_of(key, shape, shards, -0.22, 0.18) * result
    return jnp.clip(result, min=-most, max=most).astype(kind)


def setup_inputs(seed: int = 0) -> dict:
    streams_of = jax.random.split(jax.random.key(seed), 8)
    query = bell_draw(streams_of[0], (SEQLEN, QH * DH), 1.0, 6.0, ((0, 64), (1, 4)))
    key_rows = bell_draw(streams_of[1], (SEQLEN, DH), 1.0, 6.0, ((0, 64),))
    head_value_rows = bell_draw(streams_of[2], (SEQLEN, DH), 1.0, 6.0, ((0, 64),))
    output = bell_draw(streams_of[3], (SEQLEN, QH * DH), 1.0, 6.0, ((0, 64), (1, 4)))
    out_grad = bell_draw(streams_of[4], (SEQLEN, QH * DH), 0.1, 0.59765625, ((0, 64), (1, 4)))
    logsumexp = draw_logsumexp(jax.random.fold_in(streams_of[7], 71), 0)
    block_pos = draw_block_pos(jax.random.fold_in(streams_of[7], 71), 0)
    return {"query": query, "key_rows": key_rows, "head_value_rows": head_value_rows, "output": output, "out_grad": out_grad, "logsumexp": logsumexp, "block_pos": block_pos}


def lowered(x):
    return lax.optimization_barrier(x.astype(jnp.bfloat16)).astype(jnp.float32)

def reference(query, key_rows, head_value_rows, output, out_grad, logsumexp, block_pos):
    seqlen = query.shape[0]
    hdim = key_rows.shape[1]
    heads = query.shape[1] // hdim
    scale = 1.0 / math.sqrt(hdim)
    posn = (block_pos[:, None] * HALF + jnp.arange(HALF, dtype=jnp.int32)[None, :]).reshape(-1).astype(jnp.int32)
    inverse_permutation = jnp.zeros((seqlen,), jnp.int32).at[posn].set(jnp.arange(seqlen, dtype=jnp.int32))
    qsort = query[inverse_permutation].astype(jnp.float32).reshape(seqlen, heads, hdim)
    ksort = key_rows[inverse_permutation].astype(jnp.float32)
    value_sorted = head_value_rows[inverse_permutation].astype(jnp.float32)
    osort = output[inverse_permutation].astype(jnp.float32).reshape(seqlen, heads, hdim)
    dsort = out_grad[inverse_permutation].astype(jnp.float32).reshape(seqlen, heads, hdim)
    lsort = logsumexp[:, inverse_permutation]
    delta = lax.optimization_barrier(jnp.sum(osort * dsort, axis=-1)).T
    key_running_sum = jnp.zeros((seqlen, hdim), jnp.float32)
    value_running_sum = jnp.zeros((seqlen, hdim), jnp.float32)
    query_parts = []
    block = min(512, seqlen)
    for start in range(0, seqlen, block):
        stop_position = start + block
        qpart = qsort[start:stop_position]
        dpart = dsort[start:stop_position]
        key_portion = ksort[:stop_position]
        value_portion = value_sorted[:stop_position]
        scores = jnp.einsum('thd,kd->htk', qpart, key_portion) * scale
        allowed = jnp.arange(stop_position, dtype=jnp.int32)[None, :] <= jnp.arange(start, stop_position, dtype=jnp.int32)[:, None]
        probs = jnp.where(allowed[None], jnp.exp(scores - lsort[:, start:stop_position, None]), 0.0)
        value_running_sum = value_running_sum.at[:stop_position].add(jnp.einsum('htk,thd->kd', lowered(probs), dpart))
        dprobs = jnp.einsum('thd,kd->htk', dpart, value_portion)
        dscores = lowered(probs * (dprobs - delta[:, start:stop_position, None]))
        query_parts.append(jnp.einsum('htk,kd->thd', dscores, key_portion))
        key_running_sum = key_running_sum.at[:stop_position].add(jnp.einsum('htk,thd->kd', dscores, qpart))
    query_grad = (jnp.concatenate(query_parts, axis=0) * scale).reshape(seqlen, heads * hdim)[posn]
    key_grad = (key_running_sum * scale)[posn]
    value_grad = value_running_sum[posn]
    return (query_grad.astype(jnp.bfloat16), key_grad.astype(jnp.bfloat16), value_grad.astype(jnp.bfloat16))
```

```python
import functools
import math

import jax
import jax.numpy as jnp
from jax import lax
from jax.experimental import pallas as pl
from jax.experimental.pallas import tpu as pltpu
from jax.sharding import Mesh
from jax.sharding import PartitionSpec as P

HEADS = ("yl", "core")
KEY_GROUP = ("z", "x")
SWAP = [(0, 1), (1, 0)]
STEPS = [
    ("yl", SWAP),
    ("yh", SWAP),
    (("yh", "yl"), [(0, 3), (1, 2), (2, 1), (3, 0)]),
]
HALF = 128
DH = 128
PART = HALF // 4
SHARDS = 32
BLOCKS = 2 * SHARDS
KEYS = BLOCKS * PART
QROWS = 4 * HALF * 2 + 32
KROWS = 4 * PART + 8
SPAN = 8
CHUNK = SPAN * PART
VMEM_BYTES = 60 << 20
LOG2E = math.log2(math.e)
SCALE = 1.0 / math.sqrt(DH)
NT = (((1,), (1,)), ((), ()))
NN = (((1,), (0,)), ((), ()))


def dot(a, b, dims):
    return lax.dot_general(a, b, dims, preferred_element_type=jnp.float32)


def pack_kernel(block_pos, *refs):
    sources, (qmsg, kmsg), (query, key, value, output, grad, lse), sems = (
        refs[:6],
        refs[6:8],
        refs[8:14],
        refs[14],
    )
    copies = [
        pltpu.make_async_copy(src, dst, sems.at[i])
        for i, (src, dst) in enumerate(zip(sources, (query, key, value, output, grad, lse)))
    ]
    for copy in copies:
        copy.start()
    for copy in copies:
        copy.wait()
    rows = []
    drows = []
    for hb in range(2):
        for h in range(2):
            part = (slice(hb * HALF, (hb + 1) * HALF), slice(h * DH, (h + 1) * DH))
            place = (hb * 2 + h) * HALF
            qmsg[place : place + HALF, :] = query[part]
            qmsg[4 * HALF + place : 4 * HALF + place + HALF, :] = grad[part]
            prod = output[part].astype(jnp.float32) * grad[part].astype(jnp.float32)
            drows.append(jnp.sum(prod.T, axis=0, keepdims=True))
            rows.append(lse[h : h + 1, hb * HALF : (hb + 1) * HALF] * LOG2E)
    exact = jnp.concatenate(rows + drows, axis=0)
    high = exact.astype(jnp.bfloat16)
    rest = exact - high.astype(jnp.float32)
    mid = rest.astype(jnp.bfloat16)
    low = (rest - mid.astype(jnp.float32)).astype(jnp.bfloat16)
    lane = lax.broadcasted_iota(jnp.int32, (8, 128), 1)
    places = jnp.where(lane == 0, block_pos[0], block_pos[1]).astype(jnp.float32)
    extra = [v.astype(jnp.float32) for v in (high, mid, low)] + [places]
    qmsg[8 * HALF :, :] = jnp.concatenate(extra, axis=0).astype(jnp.bfloat16)

    quarter = lax.axis_index(HEADS)
    block = []
    for array in (key, value):
        for hb in range(2):
            start = pl.multiple_of(hb * HALF + quarter * PART, PART)
            block.append(array[pl.ds(start, PART), :])
    message = jnp.concatenate(block, axis=0)
    for d in range(SHARDS):
        kmsg[d, : 4 * PART, :] = message
        kmsg[d, 4 * PART :, :] = places.astype(jnp.bfloat16)


def tile_kernel(info, *refs):
    sources = refs[:9]
    dqmine, dqother, dkv = refs[9:12]
    (qs_all, kall, table, order, spos, cum, ks, vs, kst, dks, dvs, lrow, drow, dqt) = refs[12:26]
    sems = refs[26]
    places = [qs_all.at[d] for d in (0, 2, 4, 6, 1, 3, 5, 7)] + [kall]
    copies = [
        pltpu.make_async_copy(src, dst, sems.at[i])
        for i, (src, dst) in enumerate(zip(sources, places))
    ]
    for copy in reversed(copies):
        copy.start()
    quarter = lax.axis_index(HEADS)

    def clear(i, _):
        table[i] = -1
        return 0

    lax.fori_loop(0, 2 * BLOCKS, clear, 0, unroll=8)

    def enter(i, _):
        table[info[i]] = i
        return 0

    lax.fori_loop(0, BLOCKS, enter, 0, unroll=8)

    def scan(p, count):
        i = table[p]
        order[count] = i
        spos[count] = p
        count = count + jnp.where(i >= 0, 1, 0)
        cum[p] = count
        return count

    lax.fori_loop(0, 2 * BLOCKS, scan, 0, unroll=8)
    dks[...] = jnp.zeros_like(dks)
    dvs[...] = jnp.zeros_like(dvs)
    copies[8].wait()

    def place(r, _):
        i = order[r]
        src = pl.multiple_of((i % 2) * PART, PART)
        dst = pl.multiple_of(r * PART, PART)
        ks[pl.ds(dst, PART), :] = kall[i // 2, pl.ds(src, PART), :]
        vs[pl.ds(dst, PART), :] = kall[i // 2, pl.ds(src + 2 * PART, PART), :]
        return 0

    lax.fori_loop(0, BLOCKS, place, 0, unroll=8)
    for j in range(KEYS // CHUNK):
        span = slice(j * CHUNK, (j + 1) * CHUNK)
        kst[:, span] = ks[span, :].T
    for copy in copies[:8]:
        copy.wait()

    for d in range(8):
        extra = qs_all[d, 8 * HALF :, :].astype(jnp.float32)
        exact = extra[0:8] + extra[8:16] + extra[16:24]
        for hb in range(2):
            lrow[d, hb] = jnp.concatenate([exact[2 * hb : 2 * hb + 1], exact[2 * hb + 1 : 2 * hb + 2]], axis=1)
            drow[d, hb] = jnp.concatenate([exact[4 + 2 * hb : 5 + 2 * hb], exact[5 + 2 * hb : 6 + 2 * hb]], axis=1)

    gap = (
        lax.broadcasted_iota(jnp.int32, (PART, 2 * HALF), 0)
        + quarter * PART
        - lax.broadcasted_iota(jnp.int32, (PART, 2 * HALF), 1) % HALF
    )

    for hb4 in range(4):
        yh, hb = hb4 // 2, hb4 % 2
        qp = info[BLOCKS + hb4]
        seen = cum[qp]
        full = (seen - jnp.where(table[qp] >= 0, 1, 0)) // SPAN
        dqt[...] = jnp.zeros_like(dqt)

        def step(j, masked, yh=yh, hb=hb, qp=qp):
            span = pl.ds(pl.multiple_of(j * CHUNK, CHUNK), CHUNK)
            kc = ks[span, :]
            vc = vs[span, :]
            kct = kst[:, span]
            if masked:
                allowed = jnp.concatenate(
                    [gap <= (qp - spos[j * SPAN + i]) * HALF for i in range(SPAN)], axis=0
                )
            qs = [qs_all[yh * 4 + h, hb * 2 * HALF : (hb + 1) * 2 * HALF, :] for h in range(4)]
            gs = [qs_all[yh * 4 + h, (hb + 2) * 2 * HALF : (hb + 3) * 2 * HALF, :] for h in range(4)]
            low = []
            dlow = []
            for h in range(4):
                d = yh * 4 + h
                scores = dot(kc, qs[h], NT)
                probs = jnp.exp2(scores * (SCALE * LOG2E) - lrow[d, hb])
                if masked:
                    probs = jnp.where(allowed, probs, 0.0)
                dprobs = dot(vc, gs[h], NT)
                low.append(probs.astype(jnp.bfloat16))
                dlow.append((probs * (dprobs - drow[d, hb])).astype(jnp.bfloat16))
            low = jnp.concatenate(low, axis=1)
            dlow = jnp.concatenate(dlow, axis=1)
            dvs[span, :] += dot(low, jnp.concatenate(gs, axis=0), NN)
            dks[span, :] += dot(dlow, jnp.concatenate(qs, axis=0), NN)
            dqt[...] += dot(kct, dlow, NN)

        lax.fori_loop(0, full, lambda j, _, step=step: (step(j, False), 0)[1], 0)

        @pl.when(seen > full * SPAN)
        def _(step=step, full=full):
            step(full, True)

        for h in range(4):
            if h % 2 == 0:
                dqmine[yh * 2 + h // 2, hb] = dqt[:, h * 2 * HALF : (h + 1) * 2 * HALF]
            else:
                dqother[yh * 2 + h // 2, hb] = dqt[:, h * 2 * HALF : (h + 1) * 2 * HALF].astype(jnp.bfloat16)

    def restore(r, _):
        i = order[r]
        dst = pl.multiple_of((i % 2) * PART, PART)
        src = pl.multiple_of(r * PART, PART)
        dkv[i // 2, pl.ds(dst, PART), :] = dks[pl.ds(src, PART), :].astype(jnp.bfloat16)
        dkv[i // 2, pl.ds(dst + 2 * PART, PART), :] = dvs[pl.ds(src, PART), :].astype(jnp.bfloat16)
        return 0

    lax.fori_loop(0, BLOCKS, restore, 0, unroll=8)


VMEM = pl.BlockSpec(memory_space=pltpu.VMEM)
SMEM = pl.BlockSpec(memory_space=pltpu.SMEM)


def pack(block_pos, query, key, value, output, grad, lse):
    return pl.pallas_call(
        pack_kernel,
        out_shape=(
            jax.ShapeDtypeStruct((QROWS, DH), jnp.bfloat16),
            jax.ShapeDtypeStruct((SHARDS, KROWS, DH), jnp.bfloat16),
        ),
        in_specs=[SMEM] + [pl.BlockSpec(memory_space=pltpu.HBM)] * 6,
        out_specs=(VMEM, VMEM),
        scratch_shapes=[
            pltpu.VMEM(a.shape, a.dtype) for a in (query, key, value, output, grad, lse)
        ]
        + [pltpu.SemaphoreType.DMA((6,))],
        compiler_params=pltpu.CompilerParams(vmem_limit_bytes=VMEM_BYTES),
        name="pack",
    )(block_pos, query, key, value, output, grad, lse)


def tile(info, messages, kall):
    return pl.pallas_call(
        tile_kernel,
        out_shape=(
            jax.ShapeDtypeStruct((4, 2, DH, 2 * HALF), jnp.float32),
            jax.ShapeDtypeStruct((4, 2, DH, 2 * HALF), jnp.bfloat16),
            jax.ShapeDtypeStruct((SHARDS, 4 * PART, DH), jnp.bfloat16),
        ),
        in_specs=[SMEM] + [pl.BlockSpec(memory_space=pltpu.HBM)] * 9,
        out_specs=(VMEM, VMEM, VMEM),
        scratch_shapes=[
            pltpu.VMEM((8, QROWS, DH), jnp.bfloat16),
            pltpu.VMEM((SHARDS, KROWS, DH), jnp.bfloat16),
            pltpu.SMEM((2 * BLOCKS,), jnp.int32),
            pltpu.SMEM((2 * BLOCKS,), jnp.int32),
            pltpu.SMEM((2 * BLOCKS,), jnp.int32),
            pltpu.SMEM((2 * BLOCKS,), jnp.int32),
            pltpu.VMEM((KEYS, DH), jnp.bfloat16),
            pltpu.VMEM((KEYS, DH), jnp.bfloat16),
            pltpu.VMEM((DH, KEYS), jnp.bfloat16),
            pltpu.VMEM((KEYS, DH), jnp.float32),
            pltpu.VMEM((KEYS, DH), jnp.float32),
            pltpu.VMEM((8, 2, 1, 2 * HALF), jnp.float32),
            pltpu.VMEM((8, 2, 1, 2 * HALF), jnp.float32),
            pltpu.VMEM((DH, 8 * HALF), jnp.float32),
            pltpu.SemaphoreType.DMA((9,)),
        ],
        compiler_params=pltpu.CompilerParams(vmem_limit_bytes=VMEM_BYTES),
        cost_estimate=pl.CostEstimate(flops=6 * 10**9, bytes_accessed=6 << 20, transcendentals=5 * 10**6),
        name="tile",
    )(info, *messages, kall)


def shards(query, key_rows, head_value_rows, output, out_grad, logsumexp, block_pos):
    qmsg, kmsg = pack(block_pos, query, key_rows, head_value_rows, output, out_grad, logsumexp)
    kall = lax.all_to_all(kmsg, KEY_GROUP, 0, 0, tiled=True)
    near = [qmsg] + [lax.ppermute(qmsg, axes, route) for axes, route in STEPS]
    far = [lax.ppermute(message, "core", SWAP) for message in near]

    kpos = kall[:, 4 * PART, :2].astype(jnp.int32).reshape(BLOCKS)
    qpos = near[2][8 * HALF + 24, :2].astype(jnp.int32)
    info = jnp.concatenate([kpos, block_pos, qpos])
    dqmine, dqother, dkv = tile(info, near + far, kall)

    dq = dqmine + lax.ppermute(dqother, "core", SWAP).astype(jnp.float32)
    low = dq.astype(jnp.bfloat16)
    dq = dq[0]
    for i, (axes, route) in enumerate(STEPS):
        dq = dq + lax.ppermute(low[i + 1], axes, route).astype(jnp.float32)
    dkv = lax.all_to_all(dkv, KEY_GROUP, 0, 0, tiled=True)
    total = jnp.sum(dkv.astype(jnp.float32), axis=0)
    factor = jnp.where(jnp.arange(4 * PART) < 2 * PART, SCALE, 1.0).astype(jnp.float32)
    mine = (total * factor[:, None]).astype(jnp.bfloat16)
    quarters = lax.all_gather(mine, HEADS, tiled=False)
    quarters = quarters.reshape(4, 2, 2, PART, DH).transpose(1, 2, 0, 3, 4).reshape(2, 2 * HALF, DH)
    dq = (dq * SCALE).reshape(2, DH, 2, HALF).transpose(0, 3, 2, 1).reshape(2 * HALF, 2 * DH)
    return dq.astype(jnp.bfloat16), quarters[0], quarters[1]


def solution(mesh):
    split = Mesh(mesh.devices.reshape(8, 4, 2, 2, 2), ("z", "x", "yh", "yl", "core"))
    seq = ("z", "x", "yh")
    in_specs = (
        P(seq, HEADS),
        P(seq, None),
        P(seq, None),
        P(seq, HEADS),
        P(seq, HEADS),
        P(HEADS, seq),
        P(seq),
    )
    out_specs = (P(seq, HEADS), P(seq, None), P(seq, None))
    return jax.shard_map(shards, mesh=split, in_specs=in_specs, out_specs=out_specs, check_vma=False)
```

```python
import functools
import math

import jax
import jax.numpy as jnp
from jax import lax
from jax.experimental import pallas as pl
from jax.experimental.pallas import tpu as pltpu
from jax.sharding import Mesh
from jax.sharding import PartitionSpec as P

HEADS = ("yl", "core")
KEY_GROUP = ("z", "x")
SWAP = [(0, 1), (1, 0)]
STEPS = [
    ("yl", SWAP),
    ("yh", SWAP),
    (("yh", "yl"), [(0, 3), (1, 2), (2, 1), (3, 0)]),
]
HALF = 128
DH = 128
PART = HALF // 4
SHARDS = 32
BLOCKS = 2 * SHARDS
KEYS = BLOCKS * PART
QROWS = 4 * HALF * 2 + 32
KROWS = 4 * PART + 16
SPAN = 8
CHUNK = SPAN * PART
VMEM_BYTES = 60 << 20
LOG2E = math.log2(math.e)
SCALE = 1.0 / math.sqrt(DH)
NT = (((1,), (1,)), ((), ()))
NN = (((1,), (0,)), ((), ()))


def dot(a, b, dims):
    return lax.dot_general(a, b, dims, preferred_element_type=jnp.float32)


def fetch(sources, places, sems):
    copies = [
        pltpu.make_async_copy(src, dst, sems.at[i])
        for i, (src, dst) in enumerate(zip(sources, places))
    ]
    for copy in copies:
        copy.start()
    return copies


def place_row(block_pos):
    lane = lax.broadcasted_iota(jnp.int32, (8, 128), 1)
    return jnp.where(lane == 0, block_pos[0], block_pos[1]).astype(jnp.float32)


def pack_keys_kernel(block_pos, key_in, value_in, kmsg, key, value, sems):
    copies = fetch((key_in, value_in), (key, value), sems)
    places = place_row(block_pos)
    places = jnp.concatenate([places, places], axis=0).astype(jnp.bfloat16)
    quarter = lax.axis_index(HEADS)
    block = []
    for array, copy in zip((key, value), copies):
        copy.wait()
        for hb in range(2):
            start = pl.multiple_of(hb * HALF + quarter * PART, PART)
            block.append(array[pl.ds(start, PART), :])
    message = jnp.concatenate(block, axis=0)
    for d in range(8):
        kmsg[d, : 4 * PART, :] = message
        kmsg[d, 4 * PART :, :] = places


def pack_queries_kernel(block_pos, *refs):
    sources, qmsg, (query, grad, output, lse), sems = refs[:4], refs[4], refs[5:9], refs[9]
    for copy in fetch(sources, (query, grad, output, lse), sems):
        copy.wait()
    rows = []
    drows = []
    for hb in range(2):
        for h in range(2):
            part = (slice(hb * HALF, (hb + 1) * HALF), slice(h * DH, (h + 1) * DH))
            place = (hb * 2 + h) * HALF
            qmsg[place : place + HALF, :] = query[part]
            qmsg[4 * HALF + place : 4 * HALF + place + HALF, :] = grad[part]
            prod = output[part].astype(jnp.float32) * grad[part].astype(jnp.float32)
            drows.append(jnp.sum(prod.T, axis=0, keepdims=True))
            rows.append(lse[h : h + 1, hb * HALF : (hb + 1) * HALF] * LOG2E)
    exact = jnp.concatenate(rows + drows, axis=0)
    high = exact.astype(jnp.bfloat16)
    rest = exact - high.astype(jnp.float32)
    mid = rest.astype(jnp.bfloat16)
    low = (rest - mid.astype(jnp.float32)).astype(jnp.bfloat16)
    extra = [v.astype(jnp.float32) for v in (high, mid, low)] + [place_row(block_pos)]
    qmsg[8 * HALF :, :] = jnp.concatenate(extra, axis=0).astype(jnp.bfloat16)


def tile_kernel(info, *refs):
    messages, columns = refs[:8], refs[8:12]
    dqmine, dqother, dkv_out = refs[12:15]
    (qall, kall, dkv, table, order, spos, cum, ks, vs, kst) = refs[15:25]
    (dks, dvs, lrow, drow, dq, half, sems, done) = refs[25:]
    key_copies = fetch(columns, [kall.at[pl.ds(8 * c, 8)] for c in range(4)], sems)
    slots = (0, 2, 4, 6, 1, 3, 5, 7)
    copies = [None] * 8
    for i in (0, 4, 1, 5, 2, 6, 3, 7):
        copies[slots[i]] = pltpu.make_async_copy(messages[i], qall.at[slots[i]], sems.at[4 + i])
        copies[slots[i]].start()
    quarter = lax.axis_index(HEADS)
    x = lax.axis_index("x")

    def clear(i, _):
        table[i] = -1
        return 0

    lax.fori_loop(0, 2 * BLOCKS, clear, 0, unroll=8)

    def enter(i, _):
        table[info[i]] = i
        return 0

    lax.fori_loop(0, BLOCKS, enter, 0, unroll=8)

    def scan(p, count):
        i = table[p]
        order[count] = i
        spos[count] = p
        count = count + jnp.where(i >= 0, 1, 0)
        cum[p] = count
        return count

    lax.fori_loop(0, 2 * BLOCKS, scan, 0, unroll=8)
    dks[...] = jnp.zeros_like(dks)
    dvs[...] = jnp.zeros_like(dvs)
    dq[...] = jnp.zeros_like(dq)
    for copy in key_copies:
        copy.wait()

    def place(r, _):
        i = order[r]
        src = pl.multiple_of((i % 2) * PART, PART)
        dst = pl.multiple_of(r * PART, PART)
        ks[pl.ds(dst, PART), :] = kall[i // 2, pl.ds(src, PART), :]
        vs[pl.ds(dst, PART), :] = kall[i // 2, pl.ds(src + 2 * PART, PART), :]
        return 0

    lax.fori_loop(0, BLOCKS, place, 0, unroll=8)
    for j in range(KEYS // CHUNK):
        span = slice(j * CHUNK, (j + 1) * CHUNK)
        kst[:, span] = ks[span, :].T

    def queries_ready(yh):
        for h in range(4):
            d = yh * 4 + h
            copies[d].wait()
            extra = qall[d, 8 * HALF :, :].astype(jnp.float32)
            exact = extra[0:8] + extra[8:16] + extra[16:24]
            for hb in range(2):
                for row, k in ((lrow, 2 * hb), (drow, 2 * hb + 4)):
                    row[hb, d] = jnp.concatenate([exact[k : k + 1], exact[k + 1 : k + 2]], axis=1)

    gap = (
        lax.broadcasted_iota(jnp.int32, (PART, 2 * HALF), 0)
        + quarter * PART
        - lax.broadcasted_iota(jnp.int32, (PART, 2 * HALF), 1) % HALF
    )

    def dq_out(hb4):
        yh, hb = hb4 // 2, hb4 % 2
        pieces = []
        for h in range(4):
            src = dq.at[hb4, :, pl.ds(h * 2 * HALF, 2 * HALF)] if h % 2 == 0 else half.at[hb4, h // 2]
            dst = (dqmine, dqother)[h % 2].at[yh * 2 + h // 2, hb]
            pieces.append(pltpu.make_async_copy(src, dst, done.at[hb4 * 4 + h]))
        return pieces

    def half_block(hb4, _):
        yh, hb = hb4 // 2, hb4 % 2
        for now in range(2):
            pl.when(hb4 == 2 * now)(functools.partial(queries_ready, now))
        qp = info[BLOCKS + hb4]
        seen = cum[qp]
        full = (seen - jnp.where(table[qp] >= 0, 1, 0)) // SPAN
        rest = seen - full * SPAN
        qrow = pl.multiple_of(hb * 2 * HALF, 2 * HALF)
        grow = pl.multiple_of((hb + 2) * 2 * HALF, 2 * HALF)

        def step(j, count, masked):
            span = pl.ds(pl.multiple_of(j * CHUNK, CHUNK), count * PART)
            kc = ks[span, :]
            vc = vs[span, :]
            if masked:
                allowed = jnp.concatenate(
                    [gap <= (qp - spos[j * SPAN + i]) * HALF for i in range(count)], axis=0
                )
            qs = [qall[yh * 4 + h, pl.ds(qrow, 2 * HALF), :] for h in range(4)]
            gs = [qall[yh * 4 + h, pl.ds(grow, 2 * HALF), :] for h in range(4)]
            low = []
            dlow = []
            for h in range(4):
                d = yh * 4 + h
                scores = dot(kc, qs[h], NT)
                probs = jnp.exp2(scores * (SCALE * LOG2E) - lrow[hb, d])
                if masked:
                    probs = jnp.where(allowed, probs, 0.0)
                dprobs = dot(vc, gs[h], NT)
                low.append(probs.astype(jnp.bfloat16))
                dlow.append((probs * (dprobs - drow[hb, d])).astype(jnp.bfloat16))
            low = jnp.concatenate(low, axis=1)
            dlow = jnp.concatenate(dlow, axis=1)
            dvs[span, :] += dot(low, jnp.concatenate(gs, axis=0), NN)
            dks[span, :] += dot(dlow, jnp.concatenate(qs, axis=0), NN)
            dq[hb4] += dot(kst[:, span], dlow, NN)

        def body(j, _):
            step(2 * j, SPAN, False)
            step(2 * j + 1, SPAN, False)
            return 0

        lax.fori_loop(0, full // 2, body, 0)

        @pl.when(full % 2 == 1)
        def _():
            step(full - 1, SPAN, False)

        @pl.when(rest > SPAN // 2)
        def _():
            step(full, SPAN, True)

        @pl.when((rest > 0) & (rest <= SPAN // 2))
        def _():
            step(full, SPAN // 2, True)

        for h in (1, 3):
            half[hb4, h // 2] = dq[hb4, :, h * 2 * HALF : (h + 1) * 2 * HALF].astype(jnp.bfloat16)
        for copy in dq_out(hb4):
            copy.start()
        return 0

    lax.fori_loop(0, 4, half_block, 0)

    def restore(r, _):
        i = order[r]
        dst = pl.multiple_of((i % 2) * PART, PART)
        src = pl.multiple_of(r * PART, PART)
        shard = i // 2 % 8 * 4 + (i // 16 + x) % 4
        dkv[shard, pl.ds(dst, PART), :] = dks[pl.ds(src, PART), :].astype(jnp.bfloat16)
        dkv[shard, pl.ds(dst + 2 * PART, PART), :] = dvs[pl.ds(src, PART), :].astype(jnp.bfloat16)
        return 0

    lax.fori_loop(0, BLOCKS, restore, 0, unroll=8)
    copy = pltpu.make_async_copy(dkv, dkv_out, sems.at[0])
    copy.start()
    for hb4 in range(4):
        for piece in dq_out(hb4):
            piece.wait()
    copy.wait()


VMEM = pl.BlockSpec(memory_space=pltpu.VMEM)
SMEM = pl.BlockSpec(memory_space=pltpu.SMEM)
HBM = pl.BlockSpec(memory_space=pltpu.HBM)


def pack(kernel, shape, block_pos, *arrays):
    return pl.pallas_call(
        kernel,
        out_shape=jax.ShapeDtypeStruct(shape, jnp.bfloat16),
        in_specs=[SMEM] + [HBM] * len(arrays),
        out_specs=VMEM,
        scratch_shapes=[pltpu.VMEM(a.shape, a.dtype) for a in arrays]
        + [pltpu.SemaphoreType.DMA((len(arrays),))],
        compiler_params=pltpu.CompilerParams(vmem_limit_bytes=VMEM_BYTES),
        name="pack",
    )(block_pos, *arrays)


def tile(info, messages, columns):
    return pl.pallas_call(
        tile_kernel,
        out_shape=(
            jax.ShapeDtypeStruct((4, 2, DH, 2 * HALF), jnp.float32),
            jax.ShapeDtypeStruct((4, 2, DH, 2 * HALF), jnp.bfloat16),
            jax.ShapeDtypeStruct((SHARDS, 4 * PART, DH), jnp.bfloat16),
        ),
        in_specs=[SMEM] + [HBM] * 12,
        out_specs=(HBM, HBM, HBM),
        scratch_shapes=[
            pltpu.VMEM((8, QROWS, DH), jnp.bfloat16),
            pltpu.VMEM((SHARDS, KROWS, DH), jnp.bfloat16),
            pltpu.VMEM((SHARDS, 4 * PART, DH), jnp.bfloat16),
            pltpu.SMEM((2 * BLOCKS,), jnp.int32),
            pltpu.SMEM((2 * BLOCKS,), jnp.int32),
            pltpu.SMEM((2 * BLOCKS,), jnp.int32),
            pltpu.SMEM((2 * BLOCKS,), jnp.int32),
            pltpu.VMEM((KEYS, DH), jnp.bfloat16),
            pltpu.VMEM((KEYS, DH), jnp.bfloat16),
            pltpu.VMEM((DH, KEYS), jnp.bfloat16),
            pltpu.VMEM((KEYS, DH), jnp.float32),
            pltpu.VMEM((KEYS, DH), jnp.float32),
            pltpu.VMEM((2, 8, 1, 2 * HALF), jnp.float32),
            pltpu.VMEM((2, 8, 1, 2 * HALF), jnp.float32),
            pltpu.VMEM((4, DH, 8 * HALF), jnp.float32),
            pltpu.VMEM((4, 2, DH, 2 * HALF), jnp.bfloat16),
            pltpu.SemaphoreType.DMA((12,)),
            pltpu.SemaphoreType.DMA((16,)),
        ],
        compiler_params=pltpu.CompilerParams(vmem_limit_bytes=VMEM_BYTES),
        cost_estimate=pl.CostEstimate(flops=6 * 10**9, bytes_accessed=6 << 20, transcendentals=5 * 10**6),
        name="tile",
    )(info, *messages, *columns)


def moved(distance, size):
    return [(i, (i + distance) % size) for i in range(size)]


def shards(query, key_rows, head_value_rows, output, out_grad, logsumexp, block_pos):
    kmsg = pack(pack_keys_kernel, (8, KROWS, DH), block_pos, key_rows, head_value_rows)
    qmsg = pack(pack_queries_kernel, (QROWS, DH), block_pos, query, out_grad, output, logsumexp)
    column = lax.all_to_all(kmsg, "z", 0, 0, tiled=True)
    column, qmsg = lax.optimization_barrier((column, qmsg))
    columns = [column] + [lax.ppermute(column, "x", moved(-d, 4)) for d in (2, 1, 3)]
    columns = [columns[0], columns[2], columns[1], columns[3]]
    near = [qmsg] + [lax.ppermute(qmsg, axes, route) for axes, route in STEPS]
    far = [lax.ppermute(message, "core", SWAP) for message in near]

    places = [c[:, 4 * PART, :2].reshape(16) for c in columns]
    here = jnp.concatenate([block_pos.astype(jnp.bfloat16), near[2][8 * HALF + 24, :2]])
    info = jnp.concatenate(places + [here]).astype(jnp.int32)
    dqmine, dqother, dkv = tile(info, near + far, columns)

    dq = dqmine + lax.ppermute(dqother, "core", SWAP).astype(jnp.float32)
    low = dq.astype(jnp.bfloat16)
    dq = dq[0]
    for i, (axes, route) in enumerate(STEPS):
        dq = dq + lax.ppermute(low[i + 1], axes, route).astype(jnp.float32)
    dkv = lax.all_to_all(dkv, KEY_GROUP, 0, 0, tiled=True)
    total = jnp.sum(dkv.astype(jnp.float32), axis=0)
    factor = jnp.where(jnp.arange(4 * PART) < 2 * PART, SCALE, 1.0).astype(jnp.float32)
    mine = (total * factor[:, None]).astype(jnp.bfloat16)
    quarters = lax.all_gather(mine, HEADS, tiled=False)
    quarters = quarters.reshape(4, 2, 2, PART, DH).transpose(1, 2, 0, 3, 4).reshape(2, 2 * HALF, DH)
    dq = (dq * SCALE).reshape(2, DH, 2, HALF).transpose(0, 3, 2, 1).reshape(2 * HALF, 2 * DH)
    return dq.astype(jnp.bfloat16), quarters[0], quarters[1]


def solution(mesh):
    split = Mesh(mesh.devices.reshape(8, 4, 2, 2, 2), ("z", "x", "yh", "yl", "core"))
    seq = ("z", "x", "yh")
    in_specs = (
        P(seq, HEADS),
        P(seq, None),
        P(seq, None),
        P(seq, HEADS),
        P(seq, HEADS),
        P(HEADS, seq),
        P(seq),
    )
    out_specs = (P(seq, HEADS), P(seq, None), P(seq, None))
    return jax.shard_map(shards, mesh=split, in_specs=in_specs, out_specs=out_specs, check_vma=False)
```

```python
import functools
import math

import jax
import jax.numpy as jnp
from jax import lax
from jax.experimental import pallas as pl
from jax.experimental.pallas import tpu as pltpu
from jax.sharding import Mesh
from jax.sharding import PartitionSpec as P

HEADS = ("yl", "core")
KEY_GROUP = ("z", "x")
SWAP = [(0, 1), (1, 0)]
STEPS = [
    ("yl", SWAP),
    ("yh", SWAP),
    (("yh", "yl"), [(0, 3), (1, 2), (2, 1), (3, 0)]),
]
HALF = 128
DH = 128
PART = HALF // 4
SHARDS = 32
BLOCKS = 2 * SHARDS
KEYS = BLOCKS * PART
QROWS = 4 * HALF * 2 + 32
KROWS = 4 * PART + 16
SPAN = 8
CHUNK = SPAN * PART
VMEM_BYTES = 60 << 20
LOG2E = math.log2(math.e)
SCALE = 1.0 / math.sqrt(DH)
NT = (((1,), (1,)), ((), ()))
NN = (((1,), (0,)), ((), ()))


def dot(a, b, dims):
    return lax.dot_general(a, b, dims, preferred_element_type=jnp.float32)


def fetch(sources, places, sems):
    copies = [
        pltpu.make_async_copy(src, dst, sems.at[i])
        for i, (src, dst) in enumerate(zip(sources, places))
    ]
    for copy in copies:
        copy.start()
    return copies


def place_row(block_pos):
    lane = lax.broadcasted_iota(jnp.int32, (8, 128), 1)
    return jnp.where(lane == 0, block_pos[0], block_pos[1]).astype(jnp.float32)


def pack_keys_kernel(block_pos, key_in, value_in, kmsg, key, value, sems):
    copies = fetch((key_in, value_in), (key, value), sems)
    places = place_row(block_pos)
    places = jnp.concatenate([places, places], axis=0).astype(jnp.bfloat16)
    quarter = lax.axis_index(HEADS)
    block = []
    for array, copy in zip((key, value), copies):
        copy.wait()
        for hb in range(2):
            start = pl.multiple_of(hb * HALF + quarter * PART, PART)
            block.append(array[pl.ds(start, PART), :])
    message = jnp.concatenate(block, axis=0)
    for d in range(8):
        kmsg[d, : 4 * PART, :] = message
        kmsg[d, 4 * PART :, :] = places


def pack_queries_kernel(block_pos, *refs):
    sources, qmsg, (query, grad, output, lse), sems = refs[:4], refs[4], refs[5:9], refs[9]
    for copy in fetch(sources, (query, grad, output, lse), sems):
        copy.wait()
    rows = []
    drows = []
    for hb in range(2):
        for h in range(2):
            part = (slice(hb * HALF, (hb + 1) * HALF), slice(h * DH, (h + 1) * DH))
            place = (hb * 2 + h) * HALF
            qmsg[place : place + HALF, :] = query[part]
            qmsg[4 * HALF + place : 4 * HALF + place + HALF, :] = grad[part]
            prod = output[part].astype(jnp.float32) * grad[part].astype(jnp.float32)
            drows.append(jnp.sum(prod.T, axis=0, keepdims=True))
            rows.append(lse[h : h + 1, hb * HALF : (hb + 1) * HALF] * LOG2E)
    exact = jnp.concatenate(rows + drows, axis=0)
    high = exact.astype(jnp.bfloat16)
    rest = exact - high.astype(jnp.float32)
    mid = rest.astype(jnp.bfloat16)
    low = (rest - mid.astype(jnp.float32)).astype(jnp.bfloat16)
    extra = [v.astype(jnp.float32) for v in (high, mid, low)] + [place_row(block_pos)]
    qmsg[8 * HALF :, :] = jnp.concatenate(extra, axis=0).astype(jnp.bfloat16)


def tile_kernel(info, *refs):
    messages, columns = refs[:8], refs[8:12]
    dqmine, dqother, dkv_out = refs[12:15]
    (qall, kall, dkv, table, order, rank, spos, cum, ks, vs, kst) = refs[15:26]
    (dks, dvs, lrow, drow, dq, half, sems, done) = refs[26:]
    key_copies = fetch(columns, [kall.at[pl.ds(8 * c, 8)] for c in range(4)], sems)
    slots = (0, 2, 4, 6, 1, 3, 5, 7)
    copies = [None] * 8
    for i in (0, 4, 1, 5, 2, 6, 3, 7):
        copies[slots[i]] = pltpu.make_async_copy(messages[i], qall.at[slots[i]], sems.at[4 + i])
        copies[slots[i]].start()
    quarter = lax.axis_index(HEADS)
    x = lax.axis_index("x")

    def clear(i, _):
        table[i] = -1
        return 0

    lax.fori_loop(0, 2 * BLOCKS, clear, 0, unroll=8)

    def enter(i, _):
        table[info[i]] = i
        return 0

    lax.fori_loop(0, BLOCKS, enter, 0, unroll=8)

    def scan(p, count):
        i = table[p]
        order[count] = i
        rank[jnp.where(i >= 0, i, BLOCKS)] = count
        spos[count] = p
        count = count + jnp.where(i >= 0, 1, 0)
        cum[p] = count
        return count

    lax.fori_loop(0, 2 * BLOCKS, scan, 0, unroll=8)
    dks[...] = jnp.zeros_like(dks)
    dvs[...] = jnp.zeros_like(dvs)
    dq[...] = jnp.zeros_like(dq)
    for copy in key_copies:
        copy.wait()

    def place(r, _):
        i = order[r]
        src = pl.multiple_of((i % 2) * PART, PART)
        dst = pl.multiple_of(r * PART, PART)
        ks[pl.ds(dst, PART), :] = kall[i // 2, pl.ds(src, PART), :]
        vs[pl.ds(dst, PART), :] = kall[i // 2, pl.ds(src + 2 * PART, PART), :]
        return 0

    lax.fori_loop(0, BLOCKS, place, 0, unroll=8)
    for j in range(KEYS // CHUNK):
        span = slice(j * CHUNK, (j + 1) * CHUNK)
        kst[:, span] = ks[span, :].T

    def queries_ready(yh):
        for h in range(4):
            d = yh * 4 + h
            copies[d].wait()
            extra = qall[d, 8 * HALF :, :].astype(jnp.float32)
            exact = extra[0:8] + extra[8:16] + extra[16:24]
            for hb in range(2):
                for row, k in ((lrow, 2 * hb), (drow, 2 * hb + 4)):
                    row[hb, d] = jnp.concatenate([exact[k : k + 1], exact[k + 1 : k + 2]], axis=1)

    gap = (
        lax.broadcasted_iota(jnp.int32, (PART, 2 * HALF), 0)
        + quarter * PART
        - lax.broadcasted_iota(jnp.int32, (PART, 2 * HALF), 1) % HALF
    )

    def dq_out(hb4):
        yh, hb = hb4 // 2, hb4 % 2
        pieces = []
        for h in range(4):
            src = dq.at[hb4, :, pl.ds(h * 2 * HALF, 2 * HALF)] if h % 2 == 0 else half.at[hb4, h // 2]
            dst = (dqmine, dqother)[h % 2].at[yh * 2 + h // 2, hb]
            pieces.append(pltpu.make_async_copy(src, dst, done.at[hb4 * 4 + h]))
        return pieces

    def half_block(hb4, _):
        yh, hb = hb4 // 2, hb4 % 2
        for now in range(2):
            pl.when(hb4 == 2 * now)(functools.partial(queries_ready, now))
        qp = info[BLOCKS + hb4]
        seen = cum[qp]
        full = (seen - jnp.where(table[qp] >= 0, 1, 0)) // SPAN
        rest = seen - full * SPAN
        qrow = pl.multiple_of(hb * 2 * HALF, 2 * HALF)
        grow = pl.multiple_of((hb + 2) * 2 * HALF, 2 * HALF)

        def step(j, count, masked):
            span = pl.ds(pl.multiple_of(j * CHUNK, CHUNK), count * PART)
            kc = ks[span, :]
            vc = vs[span, :]
            if masked:
                allowed = jnp.concatenate(
                    [gap <= (qp - spos[j * SPAN + i]) * HALF for i in range(count)], axis=0
                )
            qs = [qall[yh * 4 + h, pl.ds(qrow, 2 * HALF), :] for h in range(4)]
            gs = [qall[yh * 4 + h, pl.ds(grow, 2 * HALF), :] for h in range(4)]
            low = []
            dlow = []
            for h in range(4):
                d = yh * 4 + h
                scores = dot(kc, qs[h], NT)
                probs = jnp.exp2(scores * (SCALE * LOG2E) - lrow[hb, d])
                if masked:
                    probs = jnp.where(allowed, probs, 0.0)
                dprobs = dot(vc, gs[h], NT)
                low.append(probs.astype(jnp.bfloat16))
                dlow.append((probs * (dprobs - drow[hb, d])).astype(jnp.bfloat16))
            low = jnp.concatenate(low, axis=1)
            dlow = jnp.concatenate(dlow, axis=1)
            dvs[span, :] += dot(low, jnp.concatenate(gs, axis=0), NN)
            dks[span, :] += dot(dlow, jnp.concatenate(qs, axis=0), NN)
            dq[hb4] += dot(kst[:, span], dlow, NN)

        def body(j, _):
            step(2 * j, SPAN, False)
            step(2 * j + 1, SPAN, False)
            return 0

        lax.fori_loop(0, full // 2, body, 0)

        @pl.when(full % 2 == 1)
        def _():
            step(full - 1, SPAN, False)

        @pl.when(rest > SPAN // 2)
        def _():
            step(full, SPAN, True)

        @pl.when((rest > 0) & (rest <= SPAN // 2))
        def _():
            step(full, SPAN // 2, True)

        for h in (1, 3):
            half[hb4, h // 2] = dq[hb4, :, h * 2 * HALF : (h + 1) * 2 * HALF].astype(jnp.bfloat16)
        for copy in dq_out(hb4):
            copy.start()
        return 0

    lax.fori_loop(0, 4, half_block, 0)

    back = []
    for c in range(4):

        def restore(i, _):
            src = pl.multiple_of(rank[i] * PART, PART)
            dst = pl.multiple_of((i % 2) * PART, PART)
            shard = i // 2
            dkv[shard, pl.ds(dst, PART), :] = dks[pl.ds(src, PART), :].astype(jnp.bfloat16)
            dkv[shard, pl.ds(dst + 2 * PART, PART), :] = dvs[pl.ds(src, PART), :].astype(jnp.bfloat16)
            return 0

        lax.fori_loop(16 * c, 16 * c + 16, restore, 0, unroll=8)
        back.append(
            pltpu.make_async_copy(
                dkv.at[pl.ds(8 * c, 8)], dkv_out.at[:, (x + c) % 4], sems.at[c]
            )
        )
        back[-1].start()
    for hb4 in range(4):
        for piece in dq_out(hb4):
            piece.wait()
    for copy in back:
        copy.wait()


VMEM = pl.BlockSpec(memory_space=pltpu.VMEM)
SMEM = pl.BlockSpec(memory_space=pltpu.SMEM)
HBM = pl.BlockSpec(memory_space=pltpu.HBM)


def pack(kernel, shape, block_pos, *arrays):
    return pl.pallas_call(
        kernel,
        out_shape=jax.ShapeDtypeStruct(shape, jnp.bfloat16),
        in_specs=[SMEM] + [HBM] * len(arrays),
        out_specs=VMEM,
        scratch_shapes=[pltpu.VMEM(a.shape, a.dtype) for a in arrays]
        + [pltpu.SemaphoreType.DMA((len(arrays),))],
        compiler_params=pltpu.CompilerParams(vmem_limit_bytes=VMEM_BYTES),
        name="pack",
    )(block_pos, *arrays)


def tile(info, messages, columns):
    return pl.pallas_call(
        tile_kernel,
        out_shape=(
            jax.ShapeDtypeStruct((4, 2, DH, 2 * HALF), jnp.float32),
            jax.ShapeDtypeStruct((4, 2, DH, 2 * HALF), jnp.bfloat16),
            jax.ShapeDtypeStruct((8, 4, 4 * PART, DH), jnp.bfloat16),
        ),
        in_specs=[SMEM] + [HBM] * 12,
        out_specs=(HBM, HBM, HBM),
        scratch_shapes=[
            pltpu.VMEM((8, QROWS, DH), jnp.bfloat16),
            pltpu.VMEM((SHARDS, KROWS, DH), jnp.bfloat16),
            pltpu.VMEM((SHARDS, 4 * PART, DH), jnp.bfloat16),
            pltpu.SMEM((2 * BLOCKS,), jnp.int32),
            pltpu.SMEM((2 * BLOCKS,), jnp.int32),
            pltpu.SMEM((2 * BLOCKS,), jnp.int32),
            pltpu.SMEM((2 * BLOCKS,), jnp.int32),
            pltpu.SMEM((2 * BLOCKS,), jnp.int32),
            pltpu.VMEM((KEYS, DH), jnp.bfloat16),
            pltpu.VMEM((KEYS, DH), jnp.bfloat16),
            pltpu.VMEM((DH, KEYS), jnp.bfloat16),
            pltpu.VMEM((KEYS, DH), jnp.float32),
            pltpu.VMEM((KEYS, DH), jnp.float32),
            pltpu.VMEM((2, 8, 1, 2 * HALF), jnp.float32),
            pltpu.VMEM((2, 8, 1, 2 * HALF), jnp.float32),
            pltpu.VMEM((4, DH, 8 * HALF), jnp.float32),
            pltpu.VMEM((4, 2, DH, 2 * HALF), jnp.bfloat16),
            pltpu.SemaphoreType.DMA((12,)),
            pltpu.SemaphoreType.DMA((16,)),
        ],
        compiler_params=pltpu.CompilerParams(vmem_limit_bytes=VMEM_BYTES),
        cost_estimate=pl.CostEstimate(flops=6 * 10**9, bytes_accessed=6 << 20, transcendentals=5 * 10**6),
        name="tile",
    )(info, *messages, *columns)


def moved(distance, size):
    return [(i, (i + distance) % size) for i in range(size)]


def shards(query, key_rows, head_value_rows, output, out_grad, logsumexp, block_pos):
    kmsg = pack(pack_keys_kernel, (8, KROWS, DH), block_pos, key_rows, head_value_rows)
    qmsg = pack(pack_queries_kernel, (QROWS, DH), block_pos, query, out_grad, output, logsumexp)
    column = lax.all_to_all(kmsg, "z", 0, 0, tiled=True)
    early = lax.ppermute(qmsg, *STEPS[1])
    column, qmsg = lax.optimization_barrier((column, qmsg))
    columns = [column] + [lax.ppermute(column, "x", moved(-d, 4)) for d in (2, 1, 3)]
    columns = [columns[0], columns[2], columns[1], columns[3]]
    near = [qmsg, lax.ppermute(qmsg, *STEPS[0]), early, lax.ppermute(qmsg, *STEPS[2])]
    far = [lax.ppermute(message, "core", SWAP) for message in near]

    places = [c[:, 4 * PART, :2].reshape(16) for c in columns]
    here = jnp.concatenate([block_pos.astype(jnp.bfloat16), near[2][8 * HALF + 24, :2]])
    info = jnp.concatenate(places + [here]).astype(jnp.int32)
    dqmine, dqother, dkv = tile(info, near + far, columns)

    dq = dqmine + lax.ppermute(dqother, "core", SWAP).astype(jnp.float32)
    low = dq.astype(jnp.bfloat16)
    dq = dq[0]
    for i, (axes, route) in enumerate(STEPS):
        dq = dq + lax.ppermute(low[i + 1], axes, route).astype(jnp.float32)
    dkv = dkv.reshape(SHARDS, 4 * PART, DH)
    dkv = lax.all_to_all(dkv, KEY_GROUP, 0, 0, tiled=True)
    total = jnp.sum(dkv.astype(jnp.float32), axis=0)
    factor = jnp.where(jnp.arange(4 * PART) < 2 * PART, SCALE, 1.0).astype(jnp.float32)
    mine = (total * factor[:, None]).astype(jnp.bfloat16)
    quarters = lax.all_gather(mine, HEADS, tiled=False)
    quarters = quarters.reshape(4, 2, 2, PART, DH).transpose(1, 2, 0, 3, 4).reshape(2, 2 * HALF, DH)
    dq = (dq * SCALE).reshape(2, DH, 2, HALF).transpose(0, 3, 2, 1).reshape(2 * HALF, 2 * DH)
    return dq.astype(jnp.bfloat16), quarters[0], quarters[1]


def solution(mesh):
    split = Mesh(mesh.devices.reshape(8, 4, 2, 2, 2), ("z", "x", "yh", "yl", "core"))
    seq = ("z", "x", "yh")
    in_specs = (
        P(seq, HEADS),
        P(seq, None),
        P(seq, None),
        P(seq, HEADS),
        P(seq, HEADS),
        P(HEADS, seq),
        P(seq),
    )
    out_specs = (P(seq, HEADS), P(seq, None), P(seq, None))
    return jax.shard_map(shards, mesh=split, in_specs=in_specs, out_specs=out_specs, check_vma=False)
```

```python
import functools
import math

import jax
import jax.numpy as jnp
from jax import lax
from jax.experimental import pallas as pl
from jax.experimental.pallas import tpu as pltpu
from jax.sharding import Mesh
from jax.sharding import PartitionSpec as P

HEADS = ("yl", "core")
KEY_GROUP = ("z", "x")
SWAP = [(0, 1), (1, 0)]
STEPS = [
    ("yl", SWAP),
    ("yh", SWAP),
    (("yh", "yl"), [(0, 3), (1, 2), (2, 1), (3, 0)]),
]
HALF = 128
DH = 128
PART = HALF // 4
SHARDS = 32
BLOCKS = 2 * SHARDS
KEYS = BLOCKS * PART
QROWS = 4 * HALF * 2 + 32
KROWS = 4 * PART + 8
SPAN = 8
CHUNK = SPAN * PART
VMEM_BYTES = 60 << 20
LOG2E = math.log2(math.e)
SCALE = 1.0 / math.sqrt(DH)
NT = (((1,), (1,)), ((), ()))
NN = (((1,), (0,)), ((), ()))


def dot(a, b, dims):
    return lax.dot_general(a, b, dims, preferred_element_type=jnp.float32)


def fetch(sources, places, sems):
    copies = [
        pltpu.make_async_copy(src, dst, sems.at[i])
        for i, (src, dst) in enumerate(zip(sources, places))
    ]
    for copy in copies:
        copy.start()
    return copies


def place_row(block_pos):
    lane = lax.broadcasted_iota(jnp.int32, (8, 128), 1)
    return jnp.where(lane == 0, block_pos[0], block_pos[1]).astype(jnp.float32)


def pack_keys_kernel(block_pos, key_in, value_in, kmsg, key, value, sems):
    copies = fetch((key_in, value_in), (key, value), sems)
    places = place_row(block_pos).astype(jnp.bfloat16)
    quarter = lax.axis_index(HEADS)
    block = []
    for array, copy in zip((key, value), copies):
        copy.wait()
        for hb in range(2):
            start = pl.multiple_of(hb * HALF + quarter * PART, PART)
            block.append(array[pl.ds(start, PART), :])
    message = jnp.concatenate(block, axis=0)
    for d in range(8):
        kmsg[d, : 4 * PART, :] = message
        kmsg[d, 4 * PART :, :] = places


def pack_queries_kernel(block_pos, *refs):
    sources, qmsg, (query, grad, output, lse), sems = refs[:4], refs[4], refs[5:9], refs[9]
    for copy in fetch(sources, (query, grad, output, lse), sems):
        copy.wait()
    rows = []
    drows = []
    for hb in range(2):
        for h in range(2):
            part = (slice(hb * HALF, (hb + 1) * HALF), slice(h * DH, (h + 1) * DH))
            place = (hb * 2 + h) * HALF
            qmsg[place : place + HALF, :] = query[part]
            qmsg[4 * HALF + place : 4 * HALF + place + HALF, :] = grad[part]
            prod = output[part].astype(jnp.float32) * grad[part].astype(jnp.float32)
            drows.append(jnp.sum(prod.T, axis=0, keepdims=True))
            rows.append(lse[h : h + 1, hb * HALF : (hb + 1) * HALF] * LOG2E)
    exact = jnp.concatenate(rows + drows, axis=0)
    high = exact.astype(jnp.bfloat16)
    rest = exact - high.astype(jnp.float32)
    mid = rest.astype(jnp.bfloat16)
    low = (rest - mid.astype(jnp.float32)).astype(jnp.bfloat16)
    extra = [v.astype(jnp.float32) for v in (high, mid, low)] + [place_row(block_pos)]
    qmsg[8 * HALF :, :] = jnp.concatenate(extra, axis=0).astype(jnp.bfloat16)


def tile_kernel(info, *refs):
    messages, columns = refs[:8], refs[8:12]
    dqmine, dqother, dkv_out = refs[12:15]
    (qall, kall, dkv, table, rank, spos, cum, ks, vs, kst) = refs[15:25]
    (dks, dvs, lrow, drow, dq, half, sems, done) = refs[25:]
    key_copies = fetch(columns, [kall.at[pl.ds(8 * c, 8)] for c in range(4)], sems)
    slots = (0, 2, 4, 6, 1, 3, 5, 7)
    copies = [None] * 8
    for i in (0, 4, 1, 5, 2, 6, 3, 7):
        copies[slots[i]] = pltpu.make_async_copy(messages[i], qall.at[slots[i]], sems.at[4 + i])
        copies[slots[i]].start()
    quarter = lax.axis_index(HEADS)
    x = lax.axis_index("x")

    def clear(i, _):
        table[i] = -1
        return 0

    lax.fori_loop(0, 2 * BLOCKS, clear, 0, unroll=8)

    def enter(i, _):
        table[info[i]] = i
        return 0

    lax.fori_loop(0, BLOCKS, enter, 0, unroll=8)

    def scan(p, count):
        i = table[p]
        rank[jnp.where(i >= 0, i, BLOCKS)] = count
        spos[count] = p
        count = count + jnp.where(i >= 0, 1, 0)
        cum[p] = count
        return count

    lax.fori_loop(0, 2 * BLOCKS, scan, 0, unroll=8)
    dks[...] = jnp.zeros_like(dks)
    dvs[...] = jnp.zeros_like(dvs)
    dq[...] = jnp.zeros_like(dq)

    def place(i, _):
        src = pl.multiple_of((i % 2) * PART, PART)
        dst = pl.multiple_of(rank[i] * PART, PART)
        ks[pl.ds(dst, PART), :] = kall[i // 2, pl.ds(src, PART), :]
        vs[pl.ds(dst, PART), :] = kall[i // 2, pl.ds(src + 2 * PART, PART), :]
        return 0

    for c in range(4):
        key_copies[c].wait()
        lax.fori_loop(16 * c, 16 * c + 16, place, 0, unroll=8)
    for j in range(KEYS // CHUNK):
        span = slice(j * CHUNK, (j + 1) * CHUNK)
        kst[:, span] = ks[span, :].T

    def queries_ready(yh):
        for h in range(4):
            d = yh * 4 + h
            copies[d].wait()
            extra = qall[d, 8 * HALF :, :].astype(jnp.float32)
            exact = extra[0:8] + extra[8:16] + extra[16:24]
            for hb in range(2):
                for row, k in ((lrow, 2 * hb), (drow, 2 * hb + 4)):
                    row[hb, d] = jnp.concatenate([exact[k : k + 1], exact[k + 1 : k + 2]], axis=1)

    gap = (
        lax.broadcasted_iota(jnp.int32, (PART, 2 * HALF), 0)
        + quarter * PART
        - lax.broadcasted_iota(jnp.int32, (PART, 2 * HALF), 1) % HALF
    )

    def dq_out(hb4):
        yh, hb = hb4 // 2, hb4 % 2
        pieces = []
        for h in range(4):
            src = dq.at[hb4, :, pl.ds(h * 2 * HALF, 2 * HALF)] if h % 2 == 0 else half.at[hb4, h // 2]
            dst = (dqmine, dqother)[h % 2].at[yh * 2 + h // 2, hb]
            pieces.append(pltpu.make_async_copy(src, dst, done.at[hb4 * 4 + h]))
        return pieces

    def half_block(hb4, _):
        yh, hb = hb4 // 2, hb4 % 2
        for now in range(2):
            pl.when(hb4 == 2 * now)(functools.partial(queries_ready, now))
        qp = info[BLOCKS + hb4]
        seen = cum[qp]
        full = (seen - jnp.where(table[qp] >= 0, 1, 0)) // SPAN
        rest = seen - full * SPAN
        qrow = pl.multiple_of(hb * 2 * HALF, 2 * HALF)
        grow = pl.multiple_of((hb + 2) * 2 * HALF, 2 * HALF)

        def step(j, count, masked):
            span = pl.ds(pl.multiple_of(j * CHUNK, CHUNK), count * PART)
            kc = ks[span, :]
            vc = vs[span, :]
            if masked:
                allowed = jnp.concatenate(
                    [gap <= (qp - spos[j * SPAN + i]) * HALF for i in range(count)], axis=0
                )
            qs = [qall[yh * 4 + h, pl.ds(qrow, 2 * HALF), :] for h in range(4)]
            gs = [qall[yh * 4 + h, pl.ds(grow, 2 * HALF), :] for h in range(4)]
            low = []
            dlow = []
            for h in range(4):
                d = yh * 4 + h
                scores = dot(kc, qs[h], NT)
                probs = jnp.exp2(scores * (SCALE * LOG2E) - lrow[hb, d])
                if masked:
                    probs = jnp.where(allowed, probs, 0.0)
                dprobs = dot(vc, gs[h], NT)
                low.append(probs.astype(jnp.bfloat16))
                dlow.append((probs * (dprobs - drow[hb, d])).astype(jnp.bfloat16))
            low = jnp.concatenate(low, axis=1)
            dlow = jnp.concatenate(dlow, axis=1)
            dvs[span, :] += dot(low, jnp.concatenate(gs, axis=0), NN)
            dks[span, :] += dot(dlow, jnp.concatenate(qs, axis=0), NN)
            dq[hb4] += dot(kst[:, span], dlow, NN)

        def body(j, _):
            for k in range(3):
                step(3 * j + k, SPAN, False)
            return 0

        lax.fori_loop(0, full // 3, body, 0)

        @pl.when(full % 3 == 1)
        def _():
            step(full - 1, SPAN, False)

        @pl.when(full % 3 == 2)
        def _():
            step(full - 2, SPAN, False)
            step(full - 1, SPAN, False)

        @pl.when(rest > SPAN // 2)
        def _():
            step(full, SPAN, True)

        @pl.when((rest > 0) & (rest <= SPAN // 2))
        def _():
            step(full, SPAN // 2, True)

        for h in (1, 3):
            half[hb4, h // 2] = dq[hb4, :, h * 2 * HALF : (h + 1) * 2 * HALF].astype(jnp.bfloat16)
        for copy in dq_out(hb4):
            copy.start()
        return 0

    lax.fori_loop(0, 4, half_block, 0)

    back = []
    for c in range(4):

        def restore(i, _):
            src = pl.multiple_of(rank[i] * PART, PART)
            dst = pl.multiple_of((i % 2) * PART, PART)
            shard = i // 2
            dkv[shard, pl.ds(dst, PART), :] = dks[pl.ds(src, PART), :].astype(jnp.bfloat16)
            dkv[shard, pl.ds(dst + 2 * PART, PART), :] = dvs[pl.ds(src, PART), :].astype(jnp.bfloat16)
            return 0

        lax.fori_loop(16 * c, 16 * c + 16, restore, 0, unroll=8)
        back.append(
            pltpu.make_async_copy(
                dkv.at[pl.ds(8 * c, 8)], dkv_out.at[:, (x + c) % 4], sems.at[c]
            )
        )
        back[-1].start()
    for hb4 in range(4):
        for piece in dq_out(hb4):
            piece.wait()
    for copy in back:
        copy.wait()


VMEM = pl.BlockSpec(memory_space=pltpu.VMEM)
SMEM = pl.BlockSpec(memory_space=pltpu.SMEM)
HBM = pl.BlockSpec(memory_space=pltpu.HBM)


def pack(kernel, shape, block_pos, *arrays):
    return pl.pallas_call(
        kernel,
        out_shape=jax.ShapeDtypeStruct(shape, jnp.bfloat16),
        in_specs=[SMEM] + [HBM] * len(arrays),
        out_specs=VMEM,
        scratch_shapes=[pltpu.VMEM(a.shape, a.dtype) for a in arrays]
        + [pltpu.SemaphoreType.DMA((len(arrays),))],
        compiler_params=pltpu.CompilerParams(vmem_limit_bytes=VMEM_BYTES),
        name="pack",
    )(block_pos, *arrays)


def tile(info, messages, columns):
    return pl.pallas_call(
        tile_kernel,
        out_shape=(
            jax.ShapeDtypeStruct((4, 2, DH, 2 * HALF), jnp.float32),
            jax.ShapeDtypeStruct((4, 2, DH, 2 * HALF), jnp.bfloat16),
            jax.ShapeDtypeStruct((8, 4, 4 * PART, DH), jnp.bfloat16),
        ),
        in_specs=[SMEM] + [HBM] * 12,
        out_specs=(HBM, HBM, HBM),
        scratch_shapes=[
            pltpu.VMEM((8, QROWS, DH), jnp.bfloat16),
            pltpu.VMEM((SHARDS, KROWS, DH), jnp.bfloat16),
            pltpu.VMEM((SHARDS, 4 * PART, DH), jnp.bfloat16),
            pltpu.SMEM((2 * BLOCKS,), jnp.int32),
            pltpu.SMEM((2 * BLOCKS,), jnp.int32),
            pltpu.SMEM((2 * BLOCKS,), jnp.int32),
            pltpu.SMEM((2 * BLOCKS,), jnp.int32),
            pltpu.VMEM((KEYS, DH), jnp.bfloat16),
            pltpu.VMEM((KEYS, DH), jnp.bfloat16),
            pltpu.VMEM((DH, KEYS), jnp.bfloat16),
            pltpu.VMEM((KEYS, DH), jnp.float32),
            pltpu.VMEM((KEYS, DH), jnp.float32),
            pltpu.VMEM((2, 8, 1, 2 * HALF), jnp.float32),
            pltpu.VMEM((2, 8, 1, 2 * HALF), jnp.float32),
            pltpu.VMEM((4, DH, 8 * HALF), jnp.float32),
            pltpu.VMEM((4, 2, DH, 2 * HALF), jnp.bfloat16),
            pltpu.SemaphoreType.DMA((12,)),
            pltpu.SemaphoreType.DMA((16,)),
        ],
        compiler_params=pltpu.CompilerParams(vmem_limit_bytes=VMEM_BYTES),
        cost_estimate=pl.CostEstimate(flops=6 * 10**9, bytes_accessed=6 << 20, transcendentals=5 * 10**6),
        name="tile",
    )(info, *messages, *columns)


def moved(distance, size):
    return [(i, (i + distance) % size) for i in range(size)]


def shards(query, key_rows, head_value_rows, output, out_grad, logsumexp, block_pos):
    kmsg = pack(pack_keys_kernel, (8, KROWS, DH), block_pos, key_rows, head_value_rows)
    qmsg = pack(pack_queries_kernel, (QROWS, DH), block_pos, query, out_grad, output, logsumexp)
    column = lax.all_to_all(kmsg, "z", 0, 0, tiled=True)
    early = lax.ppermute(qmsg, *STEPS[1])
    column, qmsg = lax.optimization_barrier((column, qmsg))
    columns = [column] + [lax.ppermute(column, "x", moved(-d, 4)) for d in (2, 1, 3)]
    columns = [columns[0], columns[2], columns[1], columns[3]]
    near = [qmsg, lax.ppermute(qmsg, *STEPS[0]), early, lax.ppermute(qmsg, *STEPS[2])]
    far = [lax.ppermute(message, "core", SWAP) for message in near]

    places = [c[:, 4 * PART, :2].reshape(16) for c in columns]
    here = jnp.concatenate([block_pos.astype(jnp.bfloat16), near[2][8 * HALF + 24, :2]])
    info = jnp.concatenate(places + [here]).astype(jnp.int32)
    dqmine, dqother, dkv = tile(info, near + far, columns)

    dq = dqmine + lax.ppermute(dqother, "core", SWAP).astype(jnp.float32)
    low = dq.astype(jnp.bfloat16)
    dq = dq[0]
    for i, (axes, route) in enumerate(STEPS):
        dq = dq + lax.ppermute(low[i + 1], axes, route).astype(jnp.float32)
    dkv = dkv.reshape(SHARDS, 4 * PART, DH)
    dkv = lax.all_to_all(dkv, KEY_GROUP, 0, 0, tiled=True)
    total = jnp.sum(dkv.astype(jnp.float32), axis=0)
    factor = jnp.where(jnp.arange(4 * PART) < 2 * PART, SCALE, 1.0).astype(jnp.float32)
    mine = (total * factor[:, None]).astype(jnp.bfloat16)
    quarters = lax.all_gather(mine, HEADS, tiled=False)
    quarters = quarters.reshape(4, 2, 2, PART, DH).transpose(1, 2, 0, 3, 4).reshape(2, 2 * HALF, DH)
    dq = (dq * SCALE).reshape(2, DH, 2, HALF).transpose(0, 3, 2, 1).reshape(2 * HALF, 2 * DH)
    return dq.astype(jnp.bfloat16), quarters[0], quarters[1]


def solution(mesh):
    split = Mesh(mesh.devices.reshape(8, 4, 2, 2, 2), ("z", "x", "yh", "yl", "core"))
    seq = ("z", "x", "yh")
    in_specs = (
        P(seq, HEADS),
        P(seq, None),
        P(seq, None),
        P(seq, HEADS),
        P(seq, HEADS),
        P(HEADS, seq),
        P(seq),
    )
    out_specs = (P(seq, HEADS), P(seq, None), P(seq, None))
    return jax.shard_map(shards, mesh=split, in_specs=in_specs, out_specs=out_specs, check_vma=False)
```
